32 devices in a mesh: ens: 2 (over y), lon: 4 (over z), lat: 2 (over x), lev: 2 (over core).
Axes of the slice: x: 2, y: 2, z: 4, core: 2. Of those that a mesh axis runs over, the one named last changes fastest.
Arguments:
- state: float32 [4, 24, 32, 256], P('ens', 'lev', 'lon', 'lat'), parts along dimension 0, may hold values from -6 to 6
- land_sea: int32 [24, 32, 256], P('lev', 'lon', 'lat'), may hold values 0 or 1
- east_speed: float32 [48, 32, 256], P(('ens', 'lev'), 'lon', 'lat'), parts along dimension 0, may hold values from -0.12 to 0.12
- north_speed: float32 [48, 32, 256], P(('ens', 'lev'), 'lon', 'lat'), parts along dimension 0, may hold values from -0.12 to 0.12
- w_in: float32 [6, 256], replicated, may hold values from -2.5 to 2.5
- b_in: float32 [256], replicated, may hold values from -3 to 3
- w_out: float32 [256, 2], replicated, may hold values from -0.375 to 0.375
- b_out: float32 [2], replicated, may hold values from -3 to 3
- cotangent: float32 [4, 24, 32, 256], P('ens', 'lev', 'lon', 'lat'), parts along dimension 0, may hold values from -6 to 6
Outputs:
- grad_state: float32 [4, 24, 32, 256], P('ens', 'lev', 'lon', 'lat'), parts along dimension 0
- grad_w_in: float32 [12, 256], P('ens'), parts along dimension 0
- grad_b_in: float32 [512], P('ens'), parts along dimension 0
- grad_w_out: float32 [512, 2], P('ens'), parts along dimension 0
- grad_b_out: float32 [4], P('ens'), parts along dimension 0
The draws below stay inside these ranges and needn't reach their ends.
There are 2 independent parts, one for each index of `ens`. The reference program is written for one: setup_inputs(seed, part) draws one part's arguments, and reference() takes and returns one part's arrays. A program takes and returns all parts, laid end to end along the dimension named above; an argument that names none is the same for every part. Nothing has to cross between parts.
All inputs are finite; a program needn't handle non-finite values. No bound on the sum of `land_sea` on one device may be relied on, other than what follows from the above.
Results may differ from the reference program's by a relative error of at most 0.00027.
Values sent between devices are 32-bit elements; how exact they have to be, the bound alone decides.
A program may use at most 64 MiB of HBM per device.

```python
import jax
import jax.numpy as jnp
from jax import lax

H = 256
NZ = 24
NX = 32
NY = 256


def place_ends(drawn, rng, least, high):
    spot = [jax.random.randint(jax.random.fold_in(rng, axis), (), 0, length) for axis, length in enumerate(drawn.shape)]
    widest = drawn.shape.index(max(drawn.shape))
    next_to = spot[:widest] + [(spot[widest] + 1) % drawn.shape[widest]] + spot[widest + 1:]
    return drawn.at[tuple(spot)].set(least).at[tuple(next_to)].set(high)


def steps_of(key, dims, cuts, smallest, largest):
    def one(dim, shards_of):
        steps = jax.random.uniform(jax.random.fold_in(jax.random.fold_in(key, 6), dim), (shards_of,), jnp.float32, smallest / len(cuts), largest / len(cuts))
        return jnp.repeat(jnp.exp(steps), dims[dim] // shards_of).reshape((-1,) + (1,) * (len(dims) - dim - 1))

    gain = one(*cuts[0])
    for cut in cuts[1:]:
        gain = gain * one(*cut)
    return gain


def normal_values(own_key, dims, width, bound, shards=(), dtype=jnp.bfloat16):
    drawn = jax.random.normal(own_key, dims, jnp.float32) * width
    if len(shards) > 0:
        drawn = steps_of(own_key, dims, shards, -0.22, 0.18) * drawn
    return jnp.clip(drawn, min=-bound, max=bound).astype(dtype)


def setup_inputs(seed: int = 0, part: int = 0) -> dict:
    arg_keys = jax.random.split(jax.random.key(seed), 10)
    own_keys = jax.random.split(jax.random.fold_in(arg_keys[9], part), 10)
    state = normal_values(own_keys[0], (2, NZ, NX, NY), 1.0, 6.0, ((1, 2), (2, 4), (3, 2)), jnp.float32)
    land_sea = place_ends((jax.random.randint(arg_keys[1], (NZ, NX, NY), 0, 4) < 3).astype(jnp.int32), jax.random.fold_in(arg_keys[1], 1), 0, 1)
    east_speed = jnp.clip(jax.random.uniform(own_keys[2], (NZ, NX, NY), jnp.float32, -0.12, 0.12) * steps_of(own_keys[2], (NZ, NX, NY), ((0, 2), (1, 4), (2, 2)), -0.4, 0.0), -0.12, 0.12)
    north_speed = jnp.clip(jax.random.uniform(own_keys[3], (NZ, NX, NY), jnp.float32, -0.12, 0.12) * steps_of(own_keys[3], (NZ, NX, NY), ((0, 2), (1, 4), (2, 2)), -0.4, 0.0), -0.12, 0.12)
    w_in = normal_values(arg_keys[4], (6, H), 6 ** -0.5, 2.5, (), jnp.float32)
    b_in = normal_values(arg_keys[5], (H,), 0.5, 3.0, (), jnp.float32)
    w_out = normal_values(arg_keys[6], (H, 2), H ** -0.5, 0.375, (), jnp.float32)
    b_out = normal_values(arg_keys[7], (2,), 1.0, 3.0, (), jnp.float32)
    cotangent = normal_values(own_keys[8], (2, NZ, NX, NY), 1.0, 6.0, ((1, 2), (2, 4), (3, 2)), jnp.float32)
    return dict(state=state, land_sea=land_sea, east_speed=east_speed, north_speed=north_speed, w_in=w_in, b_in=b_in, w_out=w_out, b_out=b_out, cotangent=cotangent)


HIGH = lax.Precision.HIGHEST

def mix_rates(feat, w_in, b_in, w_out, b_out):
    levels = feat.shape[1]
    flat = jnp.moveaxis(feat, 1, 0).reshape(levels, 6, -1)

    @jax.checkpoint
    def one_level(block):
        hidden = jnp.tanh(jnp.dot(w_in.T, block, precision=HIGH) + b_in[:, None])
        out = jnp.dot(w_out.T, hidden, precision=HIGH) + b_out[:, None]
        return jax.nn.sigmoid(out)
    rates = lax.map(one_level, flat)
    rates = jnp.moveaxis(rates, 1, 0).reshape(2, levels, feat.shape[2], feat.shape[3])
    return (0.08 * rates[0], 0.16 * rates[1])

def tracer_step(state_pad, aux_pad, params):

    def part(array, dz, dx, dy):
        nz = array.shape[1] - 2
        nx = array.shape[2] - 2
        ny = array.shape[3] - 2
        return array[:, 1 + dz:1 + dz + nz, 1 + dx:1 + dx + nx, 1 + dy:1 + dy + ny]
    center = part(state_pad, 0, 0, 0)
    mask = aux_pad[0:1]
    ocean = part(mask, 0, 0, 0)[0]
    east = part(aux_pad[1:2], 0, 0, 0)[0]
    north = part(aux_pad[2:3], 0, 0, 0)[0]

    def flux(dz, dx, dy):
        return part(mask, dz, dx, dy) * (part(state_pad, dz, dx, dy) - center)
    vertical = flux(1, 0, 0) + flux(-1, 0, 0)
    xplus = flux(0, 1, 0)
    xminus = flux(0, -1, 0)
    yplus = flux(0, 0, 1)
    yminus = flux(0, 0, -1)
    horizontal = xplus + xminus + yplus + yminus
    advect = jnp.maximum(east, 0.0) * xminus - jnp.minimum(east, 0.0) * xplus + jnp.maximum(north, 0.0) * yminus - jnp.minimum(north, 0.0) * yplus
    feat = jnp.concatenate([center, vertical, horizontal], 0)
    k_h, k_v = mix_rates(feat, params[0], params[1], params[2], params[3])
    return center + ocean * (k_h * horizontal + k_v * vertical + advect)

def pad_grid(field):
    wrapped = jnp.concatenate([field[..., -1:, :], field, field[..., :1, :]], axis=-2)
    return jnp.pad(wrapped, ((0, 0), (1, 1), (0, 0), (1, 1)))

def reference(state, land_sea, east_speed, north_speed, w_in, b_in, w_out, b_out, cotangent):
    aux = jnp.stack([land_sea.astype(jnp.float32), east_speed, north_speed])
    aux_pad = pad_grid(aux)

    def two_steps(start, wi, bi, wo, bo):
        params = (wi, bi, wo, bo)
        middle = tracer_step(pad_grid(start), aux_pad, params)
        return tracer_step(pad_grid(middle), aux_pad, params)
    unused, pullback = jax.vjp(two_steps, state, w_in, b_in, w_out, b_out)
    grads = pullback(cotangent)
    factor = float(NZ * NX * NY) ** (-0.5)
    return (grads[0], grads[1] * factor, grads[2] * factor, grads[3] * factor, grads[4] * factor)
```

```python
import jax
import jax.numpy as jnp
from jax import lax
from jax.experimental import pallas as pl
from jax.experimental.pallas import tpu as pltpu
from jax.sharding import PartitionSpec as P

MESH = pl.DeviceIdType.MESH
BF = jnp.bfloat16
F32 = jnp.float32
AXES = ("lev", "lon", "lat")
DIRECT = 16


def halves(x):
    hi = x.astype(BF).astype(F32)
    return hi, x - hi


def split(x):
    hi = x.astype(BF)
    return hi, (x - hi.astype(F32)).astype(BF)


def make_kernel(sizes, nz, hid, factor):
    total = sizes["lev"] * sizes["lon"] * sizes["lat"]
    groups = (AXES,) if total <= DIRECT else tuple((a,) for a in AXES)

    def group_size(group):
        n = 1
        for a in group:
            n *= sizes[a]
        return n

    def my_rank(group):
        me = 0
        for a in group:
            me = me * sizes[a] + lax.axis_index(a)
        return me

    def device_of(group, rank):
        where = {}
        for a in reversed(group):
            where[a] = lax.rem(rank, sizes[a])
            rank = rank // sizes[a]
        return where

    def kernel(state, land, east, north, cot, prm, gs, gp, *scratch):
        halo = [scratch[6 * p : 6 * p + 6] for p in range(4)]
        feats = scratch[24:26]
        nets = scratch[26:28]
        douts = scratch[28:30]
        near, rates, acc, small, slots = scratch[30:35]
        send_sem, recv_sem, sum_send, sum_recv = scratch[35:39]

        barrier = pltpu.get_barrier_semaphore()
        peers = 0
        for group in groups:
            n = group_size(group)
            me = my_rank(group)
            for d in range(1, n):
                pl.semaphore_signal(
                    barrier, inc=1, device_id=device_of(group, lax.rem(me + d, n)), device_id_type=MESH
                )
                peers += 1
        pl.semaphore_wait(barrier, peers)

        sub = lax.broadcasted_iota(jnp.int32, (1, 8, 128), 1)
        lane = lax.broadcasted_iota(jnp.int32, (1, 8, 128), 2)
        lane2 = lax.broadcasted_iota(jnp.int32, (8, 128), 1)

        def flag(cond):
            return jnp.where(cond, 1.0, 0.0).astype(F32)

        lev, lat = lax.axis_index("lev"), lax.axis_index("lat")
        ends = {
            "lev": (flag(lev > 0), flag(lev < sizes["lev"] - 1)),
            "lat": (flag(lat > 0), flag(lat < sizes["lat"] - 1)),
            "lon": (None, None),
        }

        def begin(p, zlo, zhi, xlo, xhi, ylo, yhi):
            sz, sx, sy, rz, rx, ry = halo[p]
            count = zlo.shape[0]
            sz[0] = zlo[:, 0]
            sz[1] = zhi[:, nz - 1]
            sx[0] = xlo[:, :, 0:1, :].reshape(count * nz, 1, 128)
            sx[1] = xhi[:, :, 7:8, :].reshape(count * nz, 1, 128)
            for side, field, at in ((0, ylo, 0), (1, yhi, 127)):
                packed = jnp.zeros((8, 128), F32)
                for t in range(count):
                    for z in range(nz):
                        packed = jnp.where(lane2 == t * nz + z, field[t, z][:, at : at + 1], packed)
                sy[side] = packed
            copies = []
            for k, (axis, src, dst) in enumerate((("lev", sz, rz), ("lon", sx, rx), ("lat", sy, ry))):
                n = sizes[axis]
                i = lax.axis_index(axis)
                for side in (0, 1):
                    to = lax.rem(i + (n - 1 if side == 0 else 1), n)
                    copy = pltpu.make_async_remote_copy(
                        src_ref=src.at[side],
                        dst_ref=dst.at[1 - side],
                        send_sem=send_sem.at[p, 2 * k + side],
                        recv_sem=recv_sem.at[p, 2 * k + 1 - side],
                        device_id={axis: to},
                        device_id_type=MESH,
                    )
                    copy.start()
                    copies.append(copy)
            return copies

        def finish(copies):
            for copy in copies:
                copy.wait()

        def closed(x, axis, side, close):
            return x * ends[axis][side] if close else x

        def up(p, c, close):
            rz = halo[p][3]
            return jnp.concatenate([c[:, 1:], closed(rz[1], "lev", 1, close)[:, None]], 1)

        def down(p, c, close):
            rz = halo[p][3]
            return jnp.concatenate([closed(rz[0], "lev", 0, close)[:, None], c[:, :-1]], 1)

        def lon_shift(p, c, side):
            rx = halo[p][4]
            flat = c.reshape(-1, 8, 128)
            rolled = pltpu.roll(flat, 7 if side == 1 else 1, 1)
            return jnp.where(sub == (7 if side == 1 else 0), rx[side], rolled).reshape(c.shape)

        def lat_shift(p, c, side, close):
            ry = halo[p][5]
            packed = closed(ry[side], "lat", side, close)
            flat = c.reshape(-1, 8, 128)
            edge = jnp.stack(
                [jnp.broadcast_to(packed[:, i : i + 1], (8, 128)) for i in range(flat.shape[0])]
            )
            rolled = pltpu.roll(flat, 127 if side == 1 else 1, 2)
            return jnp.where(lane == (127 if side == 1 else 0), edge, rolled).reshape(c.shape)

        def around(p, c, close):
            return (
                up(p, c, close),
                down(p, c, close),
                lon_shift(p, c, 1),
                lon_shift(p, c, 0),
                lat_shift(p, c, 1, close),
                lat_shift(p, c, 0, close),
            )

        mask = land[...].astype(F32)
        first = jnp.concatenate([state[...], mask[None]], 0)
        copies = begin(0, *((first,) * 6))

        rows = prm[...]
        w_hi, w_lo = halves(rows[0:8])
        lhs = jnp.concatenate([w_hi, w_hi, w_lo, w_lo, jnp.zeros((96, hid), F32)], 0)
        w_rows = lhs.T[:, :32].astype(BF)
        wo0, wo1 = rows[8:9], rows[9:10]
        row16 = lax.broadcasted_iota(jnp.int32, (16, hid), 0)
        six = lax.broadcasted_iota(jnp.int32, (8, hid), 0) < 6
        prods = jnp.concatenate(
            [jnp.where(six, rows[0:8] * wo0, 0.0), jnp.where(six, rows[0:8] * wo1, 0.0)], 0
        )
        outs = jnp.where(row16 == 6, wo0, 0.0) + jnp.where(row16 == 7, wo1, 0.0)
        g_lhs = jnp.concatenate(halves(prods), 0).astype(BF)
        h_lhs = jnp.concatenate(halves(outs), 0).astype(BF)
        bias0 = rows[10:11, 0:128].reshape(1, 1, 128)
        bias1 = rows[11:12, 0:128].reshape(1, 1, 128)

        finish(copies)
        m_near = around(0, first, True)
        for k in range(6):
            near[k] = m_near[k][2]

        def stencil(c, neighbours):
            flux = [near[k][None] * (neighbours[k] - c) for k in range(6)]
            return flux

        def features(step, c, neighbours):
            flux = stencil(c, neighbours)
            vertical = flux[0] + flux[1]
            horizontal = flux[2] + flux[3] + flux[4] + flux[5]
            ft = feats[step]
            for k, pair in enumerate((c, vertical, horizontal)):
                for t in range(2):
                    ft[:, 2 * k + t] = pair[t]
            ft[:, 6] = jnp.ones((nz, 8, 128), F32)
            ft[:, 7] = jnp.zeros((nz, 8, 128), F32)
            return flux

        def cell_rows(step, z):
            return jnp.swapaxes(feats[step][z], 0, 1)

        def hidden(cells):
            hi, lo = halves(cells)
            stacked = jnp.concatenate([hi, lo, hi, lo], 1).astype(BF)
            for pair in range(4):
                rhs = jnp.concatenate([stacked[2 * pair], stacked[2 * pair + 1]], 1)
                h = jnp.tanh(jnp.dot(w_rows, rhs, preferred_element_type=F32))
                g = 1.0 - h * h
                yield pair, split(h), split(g)

        def network(step):
            def level(z, carry):
                out = []
                for pair, h, g in hidden(cell_rows(step, z)):
                    res = (
                        jnp.dot(h_lhs, h[0], preferred_element_type=F32)
                        + jnp.dot(h_lhs, h[1], preferred_element_type=F32)
                        + jnp.dot(g_lhs, g[0], preferred_element_type=F32)
                        + jnp.dot(g_lhs, g[1], preferred_element_type=F32)
                    )
                    res = res[0:16] + res[16:32]
                    out += [res[:, 0:128], res[:, 128:256]]
                lower = jnp.stack([o[0:8] for o in out])
                upper = jnp.stack([o[8:16] for o in out])
                nets[step][z, 0:8] = jnp.swapaxes(lower, 0, 1)
                nets[step][z, 8:16] = jnp.swapaxes(upper, 0, 1)
                return carry

            lax.fori_loop(0, nz, level, 0)

        def sigmoids(step):
            net = nets[step]
            s0 = jax.nn.sigmoid(net[:, 6] + bias0)
            s1 = jax.nn.sigmoid(net[:, 7] + bias1)
            return s0, s1

        def winds():
            u, v = east[...], north[...]
            return (
                -jnp.minimum(u, 0.0),
                jnp.maximum(u, 0.0),
                -jnp.minimum(v, 0.0),
                jnp.maximum(v, 0.0),
            )

        c0 = state[...]
        flux = features(0, c0, [m[0:2] for m in m_near])
        wind = winds()
        advect = sum(wind[k][None] * flux[2 + k] for k in range(4))
        rates[...] = advect
        network(0)
        s0, s1 = sigmoids(0)
        ft = feats[0]
        move = jnp.stack(
            [0.08 * s0 * ft[:, 4 + t] + 0.16 * s1 * ft[:, 2 + t] + rates[t] for t in range(2)]
        )
        c1 = c0 + mask[None] * move
        copies = begin(1, *((c1,) * 6))
        finish(copies)
        features(1, c1, around(1, c1, False))
        network(1)

        def local_adjoint(step, lam):
            s0, s1 = sigmoids(step)
            ft, net = feats[step], nets[step]
            r = [mask * lam[t] for t in range(2)]
            d0 = (r[0] * ft[:, 4] + r[1] * ft[:, 5]) * (0.08 * s0 * (1.0 - s0))
            d1 = (r[0] * ft[:, 2] + r[1] * ft[:, 3]) * (0.16 * s1 * (1.0 - s1))
            douts[step][0] = d0
            douts[step][1] = d1
            back = [d0 * net[:, f] + d1 * net[:, 8 + f] for f in range(6)]
            center = jnp.stack([lam[t] + back[t] for t in range(2)])
            vert = jnp.stack([r[t] * (0.16 * s1) + back[2 + t] for t in range(2)])
            hor = [r[t] * (0.08 * s0) + back[4 + t] for t in range(2)]
            wind = winds()
            sides = [jnp.stack([hor[t] + wind[k] * r[t] for t in range(2)]) for k in range(4)]
            own = center - vert * (near[0] + near[1])[None]
            for k in range(4):
                own = own - sides[k] * near[2 + k][None]
            return own, vert, sides

        def gathered(p, own, vert, sides):
            e, w, n, s = sides
            came = (
                up(p, vert, True)
                + down(p, vert, True)
                + lon_shift(p, w, 1)
                + lon_shift(p, e, 0)
                + lat_shift(p, s, 1, True)
                + lat_shift(p, n, 0, True)
            )
            return own + mask[None] * came

        def weight_terms(step):
            row8 = lax.broadcasted_iota(jnp.int32, (8, 128), 0)

            def level(z, carry):
                cells = cell_rows(step, z)
                d0, d1 = douts[step][0, z], douts[step][1, z]
                g_rows, h_rows = [], []
                for s in range(8):
                    a = jnp.broadcast_to(d0[s : s + 1], (8, 128))
                    b = jnp.broadcast_to(d1[s : s + 1], (8, 128))
                    pair = jnp.concatenate([a * cells[s], b * cells[s]], 0)
                    g_rows.append(jnp.concatenate(halves(pair), 0))
                    pair = jnp.concatenate(
                        [jnp.where(row8 == 7, a, 0.0), jnp.where(row8 == 7, b, 0.0)], 0
                    )
                    h_rows.append(jnp.concatenate(halves(pair), 0))
                total_rows = jnp.zeros((32, hid), F32)
                for pair, h, g in hidden(cells):
                    gl = jnp.concatenate(g_rows[2 * pair : 2 * pair + 2], 1).astype(BF)
                    hl = jnp.concatenate(h_rows[2 * pair : 2 * pair + 2], 1).astype(BF)
                    for left, right in ((hl, h[0]), (hl, h[1]), (gl, g[0]), (gl, g[1])):
                        total_rows += lax.dot_general(
                            left, right, (((1,), (1,)), ((), ())), preferred_element_type=F32
                        )
                acc[...] += total_rows[0:16] + total_rows[16:32]
                return carry

            lax.fori_loop(0, nz, level, 0)

        own, vert, sides = local_adjoint(1, cot[...])
        copies = begin(2, vert, vert, sides[1], sides[0], sides[3], sides[2])
        acc[...] = jnp.zeros((16, hid), F32)
        weight_terms(1)
        finish(copies)
        lam = gathered(2, own, vert, sides)

        own, vert, sides = local_adjoint(0, lam)
        copies = begin(3, vert, vert, sides[1], sides[0], sides[3], sides[2])
        weight_terms(0)
        terms = acc[...]
        both = [jnp.sum(douts[0][o] + douts[1][o], axis=0) for o in range(2)]
        both = [jnp.sum(jnp.sum(b, axis=0, keepdims=True), axis=1, keepdims=True) for b in both]
        lane_h = lax.broadcasted_iota(jnp.int32, (1, hid), 1)
        last = jnp.where(lane_h == 0, both[0], 0.0) + jnp.where(lane_h == 1, both[1], 0.0)
        joined = jnp.concatenate(
            [
                terms[0:7] * wo0 + terms[8:15] * wo1,
                terms[7:8],
                terms[15:16],
                last,
                jnp.zeros((6, hid), F32),
            ],
            0,
        )
        small[0] = joined * factor

        used = 0
        for index, group in enumerate(groups):
            n = group_size(group)
            me = my_rank(group)
            slots[used + me] = small[index]
            out_copies = []
            for d in range(1, n):
                copy = pltpu.make_async_remote_copy(
                    src_ref=small.at[index],
                    dst_ref=slots.at[used + me],
                    send_sem=sum_send.at[used + d],
                    recv_sem=sum_recv.at[used + me],
                    device_id=device_of(group, lax.rem(me + d, n)),
                    device_id_type=MESH,
                )
                copy.start()
                out_copies.append(copy)
            if index == 0:
                finish(copies)
                gs[...] = gathered(3, own, vert, sides)
            for d in range(1, n):
                source = lax.rem(me + d, n)
                pltpu.make_async_remote_copy(
                    src_ref=small.at[index],
                    dst_ref=slots.at[used + source],
                    send_sem=sum_send.at[used + d],
                    recv_sem=sum_recv.at[used + source],
                    device_id=device_of(group, source),
                    device_id_type=MESH,
                ).wait_recv()
            for copy in out_copies:
                copy.wait_send()
            value = slots[used]
            for k in range(1, n):
                value = value + slots[used + k]
            used += n
            if index == len(groups) - 1:
                gp[...] = value
            else:
                small[index + 1] = value

    total_slots = sum(group_size(g) for g in groups)
    cell = lambda *lead: pltpu.VMEM((*lead, 8, 128), F32)
    scratch = []
    for count in (3, 2, 2, 2):
        scratch += [cell(2, count), pltpu.VMEM((2, count * nz, 1, 128), F32), cell(2)] * 2
    scratch += [cell(nz, 8)] * 2 + [cell(nz, 16)] * 2 + [cell(2, nz)] * 2
    scratch += [
        cell(6, nz),
        cell(2, nz),
        pltpu.VMEM((16, hid), F32),
        pltpu.VMEM((len(groups), 16, hid), F32),
        pltpu.VMEM((total_slots, 16, hid), F32),
        pltpu.SemaphoreType.DMA((4, 6)),
        pltpu.SemaphoreType.DMA((4, 6)),
        pltpu.SemaphoreType.DMA((total_slots,)),
        pltpu.SemaphoreType.DMA((total_slots,)),
    ]
    return kernel, scratch


def solution(mesh):
    sizes = {a: mesh.shape[a] for a in AXES}

    def per_device(state, land_sea, east_speed, north_speed, w_in, b_in, w_out, b_out, cotangent):
        nz = state.shape[1]
        hid = w_in.shape[1]
        cells = state.shape[1] * state.shape[2] * state.shape[3]
        cells *= sizes["lev"] * sizes["lon"] * sizes["lat"]
        kernel, scratch = make_kernel(sizes, nz, hid, float(cells) ** (-0.5))
        prm = jnp.concatenate(
            [
                w_in,
                b_in[None],
                jnp.zeros((1, hid), F32),
                w_out.T,
                jnp.broadcast_to(b_out[:, None], (2, hid)),
                jnp.zeros((4, hid), F32),
            ],
            0,
        )
        vmem = pl.BlockSpec(memory_space=pltpu.VMEM)
        grad, par = pl.pallas_call(
            kernel,
            out_shape=(
                jax.ShapeDtypeStruct(state.shape, F32),
                jax.ShapeDtypeStruct((16, hid), F32),
            ),
            in_specs=[vmem] * 6,
            out_specs=(vmem, vmem),
            scratch_shapes=scratch,
            compiler_params=pltpu.CompilerParams(
                collective_id=0, has_side_effects=True, vmem_limit_bytes=48 * 1024 * 1024
            ),
        )(state, land_sea, east_speed, north_speed, cotangent, prm)
        return grad, par[0:6], par[6], par[7:9].T, par[9, 0:2]

    placed = (
        P("ens", "lev", "lon", "lat"),
        P("lev", "lon", "lat"),
        P(("ens", "lev"), "lon", "lat"),
        P(("ens", "lev"), "lon", "lat"),
        P(),
        P(),
        P(),
        P(),
        P("ens", "lev", "lon", "lat"),
    )
    return jax.shard_map(
        per_device,
        mesh=mesh,
        in_specs=placed,
        out_specs=(
            P("ens", "lev", "lon", "lat"),
            P("ens", None),
            P("ens"),
            P("ens", None),
            P("ens"),
        ),
        check_vma=False,
    )
```

```python
import jax
import jax.numpy as jnp
from jax import lax
from jax.experimental import pallas as pl
from jax.experimental.pallas import tpu as pltpu
from jax.sharding import PartitionSpec as P

MESH = pl.DeviceIdType.MESH
BF = jnp.bfloat16
F32 = jnp.float32
AXES = ("lev", "lon", "lat")
DIRECT = 16


def halves(x):
    hi = x.astype(BF).astype(F32)
    return hi, x - hi


def split(x):
    hi = x.astype(BF)
    return hi, (x - hi.astype(F32)).astype(BF)


def make_kernel(sizes, nz, hid, factor):
    total = sizes["lev"] * sizes["lon"] * sizes["lat"]
    groups = (AXES,) if total <= DIRECT else tuple((a,) for a in AXES)

    def group_size(group):
        n = 1
        for a in group:
            n *= sizes[a]
        return n

    def my_rank(group):
        me = 0
        for a in group:
            me = me * sizes[a] + lax.axis_index(a)
        return me

    def device_of(group, rank):
        where = {}
        for a in reversed(group):
            where[a] = lax.rem(rank, sizes[a])
            rank = rank // sizes[a]
        return where

    def kernel(*refs):
        sources, (gs, g_in, g_bin, g_out, g_bout), scratch = refs[0:9], refs[9:14], refs[14:]
        state, land, east, north, cot, w_in, b_in, w_out, b_out = scratch[39:48]
        load_sem = scratch[48]
        loads = [
            pltpu.make_async_copy(sources[k], scratch[39 + k], load_sem.at[k]) for k in range(9)
        ]
        for load in loads:
            load.start()
        halo = [scratch[6 * p : 6 * p + 6] for p in range(4)]
        feats = scratch[24:26]
        nets = scratch[26:28]
        douts = scratch[28:30]
        near, rates, acc, small, slots = scratch[30:35]
        send_sem, recv_sem, sum_send, sum_recv = scratch[35:39]

        barrier = pltpu.get_barrier_semaphore()
        peers = 0
        for group in groups:
            n = group_size(group)
            me = my_rank(group)
            for d in range(1, n):
                pl.semaphore_signal(
                    barrier, inc=1, device_id=device_of(group, lax.rem(me + d, n)), device_id_type=MESH
                )
                peers += 1
        pl.semaphore_wait(barrier, peers)

        sub = lax.broadcasted_iota(jnp.int32, (1, 8, 128), 1)
        lane = lax.broadcasted_iota(jnp.int32, (1, 8, 128), 2)
        lane2 = lax.broadcasted_iota(jnp.int32, (8, 128), 1)

        def flag(cond):
            return jnp.where(cond, 1.0, 0.0).astype(F32)

        lev, lat = lax.axis_index("lev"), lax.axis_index("lat")
        ends = {
            "lev": (flag(lev > 0), flag(lev < sizes["lev"] - 1)),
            "lat": (flag(lat > 0), flag(lat < sizes["lat"] - 1)),
            "lon": (None, None),
        }

        def begin(p, zlo, zhi, xlo, xhi, ylo, yhi):
            sz, sx, sy, rz, rx, ry = halo[p]
            count = zlo.shape[0]
            sz[0] = zlo[:, 0]
            sz[1] = zhi[:, nz - 1]
            sx[0] = xlo[:, :, 0:1, :].reshape(count * nz, 1, 128)
            sx[1] = xhi[:, :, 7:8, :].reshape(count * nz, 1, 128)
            for side, field, at in ((0, ylo, 0), (1, yhi, 127)):
                packed = jnp.zeros((8, 128), F32)
                for t in range(count):
                    for z in range(nz):
                        packed = jnp.where(lane2 == t * nz + z, field[t, z][:, at : at + 1], packed)
                sy[side] = packed
            copies = []
            for k, (axis, src, dst) in enumerate((("lev", sz, rz), ("lon", sx, rx), ("lat", sy, ry))):
                n = sizes[axis]
                i = lax.axis_index(axis)
                for side in (0, 1):
                    to = lax.rem(i + (n - 1 if side == 0 else 1), n)
                    copy = pltpu.make_async_remote_copy(
                        src_ref=src.at[side],
                        dst_ref=dst.at[1 - side],
                        send_sem=send_sem.at[p, 2 * k + side],
                        recv_sem=recv_sem.at[p, 2 * k + 1 - side],
                        device_id={axis: to},
                        device_id_type=MESH,
                    )
                    copy.start()
                    copies.append(copy)
            return copies

        def finish(copies):
            for copy in copies:
                copy.wait()

        def closed(x, axis, side, close):
            return x * ends[axis][side] if close else x

        def up(p, c, close):
            rz = halo[p][3]
            return jnp.concatenate([c[:, 1:], closed(rz[1], "lev", 1, close)[:, None]], 1)

        def down(p, c, close):
            rz = halo[p][3]
            return jnp.concatenate([closed(rz[0], "lev", 0, close)[:, None], c[:, :-1]], 1)

        def lon_shift(p, c, side):
            rx = halo[p][4]
            flat = c.reshape(-1, 8, 128)
            rolled = pltpu.roll(flat, 7 if side == 1 else 1, 1)
            return jnp.where(sub == (7 if side == 1 else 0), rx[side], rolled).reshape(c.shape)

        def lat_shift(p, c, side, close):
            ry = halo[p][5]
            packed = closed(ry[side], "lat", side, close)
            flat = c.reshape(-1, 8, 128)
            edge = jnp.stack(
                [jnp.broadcast_to(packed[:, i : i + 1], (8, 128)) for i in range(flat.shape[0])]
            )
            rolled = pltpu.roll(flat, 127 if side == 1 else 1, 2)
            return jnp.where(lane == (127 if side == 1 else 0), edge, rolled).reshape(c.shape)

        def around(p, c, close):
            return (
                up(p, c, close),
                down(p, c, close),
                lon_shift(p, c, 1),
                lon_shift(p, c, 0),
                lat_shift(p, c, 1, close),
                lat_shift(p, c, 0, close),
            )

        loads[0].wait()
        loads[1].wait()
        mask = land[...].astype(F32)
        first = jnp.concatenate([state[...], mask[None]], 0)
        copies = begin(0, *((first,) * 6))

        for k in range(5, 9):
            loads[k].wait()
        rows = jnp.concatenate([w_in[...], b_in[...], jnp.zeros((1, hid), F32)], 0)
        w_hi, w_lo = halves(rows)
        lhs = jnp.concatenate([w_hi, w_hi, w_lo, w_lo, jnp.zeros((96, hid), F32)], 0)
        w_rows = lhs.T[:, :32].astype(BF)
        wo0, wo1 = w_out[0:1], w_out[1:2]
        row16 = lax.broadcasted_iota(jnp.int32, (16, hid), 0)
        six = lax.broadcasted_iota(jnp.int32, (8, hid), 0) < 6
        prods = jnp.concatenate(
            [jnp.where(six, rows * wo0, 0.0), jnp.where(six, rows * wo1, 0.0)], 0
        )
        outs = jnp.where(row16 == 6, wo0, 0.0) + jnp.where(row16 == 7, wo1, 0.0)
        g_lhs = jnp.concatenate(halves(prods), 0).astype(BF)
        h_lhs = jnp.concatenate(halves(outs), 0).astype(BF)
        bias0 = jnp.broadcast_to(b_out[:, 0:1], (8, 128))[None]
        bias1 = jnp.broadcast_to(b_out[:, 1:2], (8, 128))[None]

        loads[2].wait()
        loads[3].wait()
        loads[4].wait()
        finish(copies)
        m_near = around(0, first, True)
        for k in range(6):
            near[k] = m_near[k][2]

        def stencil(c, neighbours):
            flux = [near[k][None] * (neighbours[k] - c) for k in range(6)]
            return flux

        def features(step, c, neighbours):
            flux = stencil(c, neighbours)
            vertical = flux[0] + flux[1]
            horizontal = flux[2] + flux[3] + flux[4] + flux[5]
            ft = feats[step]
            for k, pair in enumerate((c, vertical, horizontal)):
                for t in range(2):
                    ft[:, 2 * k + t] = pair[t]
            ft[:, 6] = jnp.ones((nz, 8, 128), F32)
            ft[:, 7] = jnp.zeros((nz, 8, 128), F32)
            return flux

        def cell_rows(step, z):
            return jnp.swapaxes(feats[step][z], 0, 1)

        def hidden(cells):
            hi, lo = halves(cells)
            stacked = jnp.concatenate([hi, lo, hi, lo], 1).astype(BF)
            for pair in range(4):
                rhs = jnp.concatenate([stacked[2 * pair], stacked[2 * pair + 1]], 1)
                h = jnp.tanh(jnp.dot(w_rows, rhs, preferred_element_type=F32))
                g = 1.0 - h * h
                yield pair, split(h), split(g)

        def network(step):
            def level(z, carry):
                out = []
                for pair, h, g in hidden(cell_rows(step, z)):
                    res = (
                        jnp.dot(h_lhs, h[0], preferred_element_type=F32)
                        + jnp.dot(h_lhs, h[1], preferred_element_type=F32)
                        + jnp.dot(g_lhs, g[0], preferred_element_type=F32)
                        + jnp.dot(g_lhs, g[1], preferred_element_type=F32)
                    )
                    res = res[0:16] + res[16:32]
                    out += [res[:, 0:128], res[:, 128:256]]
                lower = jnp.stack([o[0:8] for o in out])
                upper = jnp.stack([o[8:16] for o in out])
                nets[step][z, 0:8] = jnp.swapaxes(lower, 0, 1)
                nets[step][z, 8:16] = jnp.swapaxes(upper, 0, 1)
                return carry

            lax.fori_loop(0, nz, level, 0)

        def sigmoids(step):
            net = nets[step]
            s0 = jax.nn.sigmoid(net[:, 6] + bias0)
            s1 = jax.nn.sigmoid(net[:, 7] + bias1)
            return s0, s1

        def winds():
            u, v = east[...], north[...]
            return (
                -jnp.minimum(u, 0.0),
                jnp.maximum(u, 0.0),
                -jnp.minimum(v, 0.0),
                jnp.maximum(v, 0.0),
            )

        c0 = state[...]
        flux = features(0, c0, [m[0:2] for m in m_near])
        wind = winds()
        advect = sum(wind[k][None] * flux[2 + k] for k in range(4))
        rates[...] = advect
        network(0)
        s0, s1 = sigmoids(0)
        ft = feats[0]
        move = jnp.stack(
            [0.08 * s0 * ft[:, 4 + t] + 0.16 * s1 * ft[:, 2 + t] + rates[t] for t in range(2)]
        )
        c1 = c0 + mask[None] * move
        copies = begin(1, *((c1,) * 6))
        finish(copies)
        features(1, c1, around(1, c1, False))
        network(1)

        def local_adjoint(step, lam):
            s0, s1 = sigmoids(step)
            ft, net = feats[step], nets[step]
            r = [mask * lam[t] for t in range(2)]
            d0 = (r[0] * ft[:, 4] + r[1] * ft[:, 5]) * (0.08 * s0 * (1.0 - s0))
            d1 = (r[0] * ft[:, 2] + r[1] * ft[:, 3]) * (0.16 * s1 * (1.0 - s1))
            douts[step][0] = d0
            douts[step][1] = d1
            back = [d0 * net[:, f] + d1 * net[:, 8 + f] for f in range(6)]
            center = jnp.stack([lam[t] + back[t] for t in range(2)])
            vert = jnp.stack([r[t] * (0.16 * s1) + back[2 + t] for t in range(2)])
            hor = [r[t] * (0.08 * s0) + back[4 + t] for t in range(2)]
            wind = winds()
            sides = [jnp.stack([hor[t] + wind[k] * r[t] for t in range(2)]) for k in range(4)]
            own = center - vert * (near[0] + near[1])[None]
            for k in range(4):
                own = own - sides[k] * near[2 + k][None]
            return own, vert, sides

        def gathered(p, own, vert, sides):
            e, w, n, s = sides
            came = (
                up(p, vert, True)
                + down(p, vert, True)
                + lon_shift(p, w, 1)
                + lon_shift(p, e, 0)
                + lat_shift(p, s, 1, True)
                + lat_shift(p, n, 0, True)
            )
            return own + mask[None] * came

        def weight_terms(step):
            row8 = lax.broadcasted_iota(jnp.int32, (8, 128), 0)

            def level(z, carry):
                cells = cell_rows(step, z)
                d0, d1 = douts[step][0, z], douts[step][1, z]
                g_rows, h_rows = [], []
                for s in range(8):
                    a = jnp.broadcast_to(d0[s : s + 1], (8, 128))
                    b = jnp.broadcast_to(d1[s : s + 1], (8, 128))
                    pair = jnp.concatenate([a * cells[s], b * cells[s]], 0)
                    g_rows.append(jnp.concatenate(halves(pair), 0))
                    pair = jnp.concatenate(
                        [jnp.where(row8 == 7, a, 0.0), jnp.where(row8 == 7, b, 0.0)], 0
                    )
                    h_rows.append(jnp.concatenate(halves(pair), 0))
                lefts, rights = [], []
                for pair, h, g in hidden(cells):
                    gl = jnp.concatenate(g_rows[2 * pair : 2 * pair + 2], 1).astype(BF)
                    hl = jnp.concatenate(h_rows[2 * pair : 2 * pair + 2], 1).astype(BF)
                    lefts += [h[0], h[1], g[0], g[1]]
                    rights += [hl, hl, gl, gl]
                acc[...] += lax.dot_general(
                    jnp.concatenate(lefts, 1),
                    jnp.concatenate(rights, 1),
                    (((1,), (1,)), ((), ())),
                    preferred_element_type=F32,
                )
                return carry

            lax.fori_loop(0, nz, level, 0)

        own, vert, sides = local_adjoint(1, cot[...])
        copies = begin(2, vert, vert, sides[1], sides[0], sides[3], sides[2])
        acc[...] = jnp.zeros((hid, 32), F32)
        weight_terms(1)
        finish(copies)
        lam = gathered(2, own, vert, sides)

        own, vert, sides = local_adjoint(0, lam)
        copies = begin(3, vert, vert, sides[1], sides[0], sides[3], sides[2])
        weight_terms(0)
        terms = jnp.concatenate([acc[...], jnp.zeros((hid, 96), F32)], 1).T
        terms = terms[0:16] + terms[16:32]
        both = [jnp.sum(douts[0][o] + douts[1][o], axis=0) for o in range(2)]
        both = [jnp.sum(jnp.sum(b, axis=0, keepdims=True), axis=1, keepdims=True) for b in both]
        lane_h = lax.broadcasted_iota(jnp.int32, (1, hid), 1)
        last = jnp.where(lane_h == 0, both[0], 0.0) + jnp.where(lane_h == 1, both[1], 0.0)
        joined = jnp.concatenate(
            [
                terms[0:7] * wo0 + terms[8:15] * wo1,
                terms[7:8],
                terms[15:16],
                last,
                jnp.zeros((6, hid), F32),
            ],
            0,
        )
        small[0] = joined * factor

        used = 0
        for index, group in enumerate(groups):
            n = group_size(group)
            me = my_rank(group)
            slots[used + me] = small[index]
            out_copies = []
            for d in range(1, n):
                copy = pltpu.make_async_remote_copy(
                    src_ref=small.at[index],
                    dst_ref=slots.at[used + me],
                    send_sem=sum_send.at[used + d],
                    recv_sem=sum_recv.at[used + me],
                    device_id=device_of(group, lax.rem(me + d, n)),
                    device_id_type=MESH,
                )
                copy.start()
                out_copies.append(copy)
            if index == 0:
                finish(copies)
                gs[...] = gathered(3, own, vert, sides)
            for d in range(1, n):
                source = lax.rem(me + d, n)
                pltpu.make_async_remote_copy(
                    src_ref=small.at[index],
                    dst_ref=slots.at[used + source],
                    send_sem=sum_send.at[used + d],
                    recv_sem=sum_recv.at[used + source],
                    device_id=device_of(group, source),
                    device_id_type=MESH,
                ).wait_recv()
            for copy in out_copies:
                copy.wait_send()
            value = slots[used]
            for k in range(1, n):
                value = value + slots[used + k]
            used += n
            if index == len(groups) - 1:
                g_in[...] = value[0:6]
                g_bin[...] = value[6:7]
                g_out[...] = value[7:9]
                g_bout[...] = value[9:10, 0:2]
            else:
                small[index + 1] = value

    total_slots = sum(group_size(g) for g in groups)
    cell = lambda *lead: pltpu.VMEM((*lead, 8, 128), F32)
    scratch = []
    for count in (3, 2, 2, 2):
        scratch += [cell(2, count), pltpu.VMEM((2, count * nz, 1, 128), F32), cell(2)] * 2
    scratch += [cell(nz, 8)] * 2 + [cell(nz, 16)] * 2 + [cell(2, nz)] * 2
    scratch += [
        cell(6, nz),
        cell(2, nz),
        pltpu.VMEM((hid, 32), F32),
        pltpu.VMEM((len(groups), 16, hid), F32),
        pltpu.VMEM((total_slots, 16, hid), F32),
        pltpu.SemaphoreType.DMA((4, 6)),
        pltpu.SemaphoreType.DMA((4, 6)),
        pltpu.SemaphoreType.DMA((total_slots,)),
        pltpu.SemaphoreType.DMA((total_slots,)),
        cell(2, nz),
        pltpu.VMEM((nz, 8, 128), jnp.int32),
        cell(nz),
        cell(nz),
        cell(2, nz),
        pltpu.VMEM((6, hid), F32),
        pltpu.VMEM((1, hid), F32),
        pltpu.VMEM((2, hid), F32),
        pltpu.VMEM((1, 2), F32),
        pltpu.SemaphoreType.DMA((9,)),
    ]
    return kernel, scratch


def hand_over(*refs):
    sem = refs[10]
    copies = [pltpu.make_async_copy(refs[k], refs[5 + k], sem.at[k]) for k in range(5)]
    for copy in copies:
        copy.start()
    for copy in copies:
        copy.wait()


def solution(mesh):
    sizes = {a: mesh.shape[a] for a in AXES}

    def per_device(state, land_sea, east_speed, north_speed, w_in, b_in, w_out, b_out, cotangent):
        nz = state.shape[1]
        hid = w_in.shape[1]
        cells = state.shape[1] * state.shape[2] * state.shape[3]
        cells *= sizes["lev"] * sizes["lon"] * sizes["lat"]
        kernel, scratch = make_kernel(sizes, nz, hid, float(cells) ** (-0.5))
        vmem = pl.BlockSpec(memory_space=pltpu.VMEM)
        shapes = (
            jax.ShapeDtypeStruct(state.shape, F32),
            jax.ShapeDtypeStruct((6, hid), F32),
            jax.ShapeDtypeStruct((1, hid), F32),
            jax.ShapeDtypeStruct((2, hid), F32),
            jax.ShapeDtypeStruct((1, 2), F32),
        )
        results = pl.pallas_call(
            kernel,
            out_shape=shapes,
            in_specs=[pl.BlockSpec(memory_space=pl.ANY)] * 9,
            out_specs=(vmem,) * 5,
            scratch_shapes=scratch,
            compiler_params=pltpu.CompilerParams(
                collective_id=0, has_side_effects=True, vmem_limit_bytes=60 * 1024 * 1024
            ),
        )(
            state,
            land_sea,
            east_speed,
            north_speed,
            cotangent,
            w_in,
            b_in[None],
            w_out.T,
            b_out[None],
        )
        anywhere = pl.BlockSpec(memory_space=pl.ANY)
        grad, g_in, g_bin, g_out, g_bout = pl.pallas_call(
            hand_over,
            out_shape=shapes,
            in_specs=[anywhere] * 5,
            out_specs=(anywhere,) * 5,
            scratch_shapes=[pltpu.SemaphoreType.DMA((5,))],
            compiler_params=pltpu.CompilerParams(vmem_limit_bytes=60 * 1024 * 1024),
        )(*results)
        return grad, g_in, g_bin[0], g_out.T, g_bout[0]

    placed = (
        P("ens", "lev", "lon", "lat"),
        P("lev", "lon", "lat"),
        P(("ens", "lev"), "lon", "lat"),
        P(("ens", "lev"), "lon", "lat"),
        P(),
        P(),
        P(),
        P(),
        P("ens", "lev", "lon", "lat"),
    )
    return jax.shard_map(
        per_device,
        mesh=mesh,
        in_specs=placed,
        out_specs=(
            P("ens", "lev", "lon", "lat"),
            P("ens", None),
            P("ens"),
            P("ens", None),
            P("ens"),
        ),
        check_vma=False,
    )
```
